256 devices in a mesh: blk: 16 (over y, x_hi, core), bulk: 16 (over z, x_lo).
Axes of the slice: x: 4 (x_hi: 2, x_lo: 2; x = x_hi * 2 + x_lo), y: 4, z: 8, core: 2. Of those that a mesh axis runs over, the one named last changes fastest.
Arguments:
- amplitudes: bfloat16 [1600, 28800], P('blk', 'bulk'), may hold values from -6 to 6
- integrals: bfloat16 [28800, 28800], P('bulk', 'blk'), may hold values from -0.03125 to 0.03125
- cd_blocks: int32 [32, 2], P('bulk'), may hold values from 0 to 29, as said below
Outputs:
- ladder: float32 [1600, 28800], P('bulk', 'blk')
The draws below stay inside these ranges and needn't reach their ends.
Inputs may be any that keep to these rules, and one draw needn't show every extreme that they name: `cd_blocks`: each row holds two virtual block numbers below 30, the first not greater than the second.
All inputs are finite; a program needn't handle non-finite values.
Results may differ from the reference program's by a relative error of at most 0.0003.
Values may be sent and summed in bfloat16 or wider, within the bound.
A program may use at most 128 MiB of HBM per device.

```python
import jax
import jax.numpy as jnp

NVB = 30
PB = 900
IJ = 1600
NP = 32
NQ = 32
N_BULK = 16


def draw_cd_blocks(key, part):
    key = jax.random.fold_in(key, 7)
    key_first, key_step = jax.random.split(key)
    first = jax.random.randint(key_first, (NQ,), 0, NVB)
    offset = jax.random.randint(key_step, (NQ,), 0, 2)
    second = jnp.minimum(first + offset, NVB - 1)
    first = first.at[0].set(0)
    second = second.at[0].set(NVB - 1)
    return jnp.stack([first, second], axis=1).astype(jnp.int32)


def steps_of(own_key, shape, pieces, low, high):
    def one(axis_at, parts):
        heights = jax.random.uniform(jax.random.fold_in(jax.random.fold_in(own_key, 6), axis_at), (parts,), jnp.float32, low / len(pieces), high / len(pieces))
        return jnp.repeat(jnp.exp(heights), shape[axis_at] // parts).reshape((-1,) + (1,) * (len(shape) - axis_at - 1))

    factor_of = one(*pieces[0])
    for cut in pieces[1:]:
        factor_of = factor_of * one(*cut)
    return factor_of


def noise(key, extent, deviation, reach, cuts=(), held_as=jnp.bfloat16):
    values = jax.random.normal(key, extent, jnp.float32) * deviation
    if len(cuts) > 0:
        values = steps_of(key, extent, cuts, -0.22, 0.18) * values
    return jnp.clip(values, min=-reach, max=reach).astype(held_as)


def setup_inputs(seed: int = 0) -> dict:
    keys = jax.random.split(jax.random.key(seed), 4)
    amplitudes = noise(keys[0], (IJ, NQ * PB), 1.0, 6.0, ((0, 16), (1, 16)))
    integrals = noise(keys[1], (NQ * PB, NP * PB), (NQ * PB) ** -0.5, 0.03125, ((0, 16), (1, 16)))
    cd_blocks = draw_cd_blocks(jax.random.fold_in(keys[3], 71), 0)
    return {"amplitudes": amplitudes, "integrals": integrals, "cd_blocks": cd_blocks}


def reference(amplitudes, integrals, cd_blocks):
    per_block = integrals.shape[0] // cd_blocks.shape[0]
    factor = 2.0 - (cd_blocks[:, 0] == cd_blocks[:, 1]).astype(jnp.float32)
    column_weight = jnp.repeat(factor, per_block)
    weighted = (amplitudes.astype(jnp.float32) * column_weight[None, :]).astype(jnp.bfloat16)
    share = integrals.shape[0] // N_BULK
    total = jnp.zeros((amplitudes.shape[0], integrals.shape[1]), jnp.float32)
    for group in range(N_BULK):
        partial_value = jnp.dot(weighted[:, group * share:(group + 1) * share], integrals[group * share:(group + 1) * share], preferred_element_type=jnp.float32)
        total = total + partial_value
    return total
```

```python
import functools

import jax
import jax.numpy as jnp
from jax import lax
from jax.experimental import pallas as pl
from jax.experimental.pallas import tpu as pltpu
from jax.sharding import PartitionSpec as P

MESH = pl.DeviceIdType.MESH
F32 = jnp.float32

DELTA = (4, 3, 5, 2, 6, 1, 7, 0)
NZ = 4
NB = 7
NX = NB - NZ
XA = (NX + 1) // 2
LANES = 128
PAD = 112
ROWS = 104
HALVES = ((0, 64), (64, 48))


def kernel(a_ref, cd_ref, b_hbm, out_ref, abuf, b_ref, part, tmp, left, zs, zr, zsx, zrx, xs, xr, xsx, xrx,
           es, er, esx, erx, fs, fr, b_sem, g_send, g_recv, z_send, z_recv, x_send, x_recv, e_send, e_recv):
    rows, depth = a_ref.shape
    tail = b_hbm.shape[1] - NB * 256
    blk, bulk = lax.axis_index("blk"), lax.axis_index("bulk")
    y, h, k = blk // 4, (blk // 2) % 2, blk % 2
    z, xl = bulk // 2, bulk % 2

    def at_y(step):
        return (((y + step + 4) % 4) * 4 + h * 2 + k, bulk)

    def at_z(step):
        return (blk, ((z + step + 8) % 8) * 2 + xl)

    up, down = at_z(1), at_z(-1)
    y_up, y_down = at_y(1), at_y(-1)
    across = (y * 4 + (1 - h) * 2 + k, bulk)
    sibling = (y * 4 + h * 2 + (1 - k), bulk)
    pair = (blk, z * 2 + (1 - xl))

    b_copy = pltpu.make_async_copy(b_hbm, b_ref, b_sem)
    b_copy.start()

    barrier = pltpu.get_barrier_semaphore()
    partners = (up, down, y_up, y_down, across, sibling, pair)
    for partner in partners:
        pl.semaphore_signal(barrier, inc=1, device_id=partner, device_id_type=MESH)

    def remote(src, dst, send, recv, target):
        return pltpu.make_async_remote_copy(
            src_ref=src, dst_ref=dst, send_sem=send, recv_sem=recv, device_id=target, device_id_type=MESH
        )

    own = [(z + d) % 8 for d in DELTA]
    dys = [(y - c // 2 + 4) % 4 for c in own]
    sames = [h == c % 2 for c in own]
    sources = [jnp.logical_and(dy == 0, same) for dy, same in zip(dys, sames)]
    p_own = sum(jnp.where(s, p, 0) for p, s in enumerate(sources))

    per_block = depth // cd_ref.shape[0]
    column = lax.broadcasted_iota(jnp.int32, (1, depth), 1)
    weight = jnp.zeros((1, depth), F32)
    for block in range(cd_ref.shape[0]):
        factor = jnp.where(cd_ref[block, 0] == cd_ref[block, 1], 1.0, 2.0).astype(F32)
        inside = jnp.logical_and(column >= block * per_block, column < (block + 1) * per_block)
        weight = jnp.where(inside, factor, weight)
    abuf[p_own, k] = jnp.zeros((PAD, depth), jnp.bfloat16)
    abuf[p_own, k, 0:rows] = (a_ref[...].astype(F32) * weight).astype(jnp.bfloat16)
    tmp[...] = jnp.zeros_like(tmp)

    pl.semaphore_wait(barrier, len(partners))

    def half(p, l, part_of):
        start, size = HALVES[part_of]
        return abuf.at[p, l, pl.ds(start, size)]

    def g_copy(p, part_of, way, target):
        ref = half(p, k, part_of)
        return remote(ref, ref, g_send.at[p, part_of, way], g_recv.at[p, k, part_of], target)

    def g_sends(p, part_of):
        dy = dys[p]
        goes_up = jnp.logical_or(dy == 0, dy == 1) if part_of == 0 else dy == 0
        goes_down = jnp.logical_or(dy == 0, dy == 3) if part_of == 1 else dy == 0
        return (
            (sources[p], g_copy(p, part_of, 0, across)),
            (goes_up, g_copy(p, part_of, 1, y_up)),
            (goes_down, g_copy(p, part_of, 2, y_down)),
            (None, g_copy(p, part_of, 3, sibling)),
        )

    def pass_on(p, part_of):
        for when, copy in g_sends(p, part_of):
            if when is None:
                copy.start()
            else:
                pl.when(when)(copy.start)

    def launch(p):
        @pl.when(sources[p])
        def _():
            for part_of in range(2):
                for _, copy in g_sends(p, part_of):
                    copy.start()

    def arrive(p):
        @pl.when(jnp.logical_not(sources[p]))
        def _():
            for part_of in range(2):
                g_copy(p, part_of, 3, sibling).wait_recv()
                dy = dys[p]
                for when, copy in g_sends(p, part_of)[1:]:
                    if when is None:
                        copy.start()
                    else:
                        pl.when(when)(copy.start)

    def arrive_sibling(p):
        for part_of in range(2):
            ref = half(p, 1 - k, part_of)
            remote(ref, ref, g_send.at[p, part_of, 3], g_recv.at[p, 1 - k, part_of], sibling).wait_recv()

    def multiply(p):
        lhs = abuf[p].reshape(2 * PAD, depth)

        def body(nb, _):
            r = jnp.dot(lhs, b_ref[:, pl.ds(pl.multiple_of(nb * 256, 256), 256)], preferred_element_type=F32)
            for l in range(2):
                for side in range(2):
                    part[p, l, nb, side * ROWS:(side + 1) * ROWS] = r[
                        l * PAD:l * PAD + ROWS, side * LANES:(side + 1) * LANES]
            return 0

        lax.fori_loop(0, NB, body, 0)
        r = jnp.dot(lhs, b_ref[:, NB * 256:], preferred_element_type=F32)
        for l in range(2):
            tmp[0:PAD, 0:tail] = r[l * PAD:(l + 1) * PAD]
            left[p, l] = tmp[...].T[0:8]

    def add(p, l, first, count, q, scale):
        factor = scale[0:8]

        def body(b, _):
            more = q[b].astype(F32).reshape(-1, 8, LANES) * factor
            v = part[p, l, first + b].reshape(-1, 8, LANES) + more
            part[p, l, first + b] = v.reshape(2 * ROWS, LANES)
            return 0

        lax.fori_loop(0, count, body, 0)

    def quantize(p, l, first, count, q, scale):
        def largest(b, m):
            v = jnp.abs(part[p, l, first + b].reshape(-1, 8, LANES))
            return jnp.maximum(m, jnp.max(v, axis=0))

        m = lax.fori_loop(0, count, largest, jnp.zeros((8, LANES), F32))
        m = jnp.maximum(m, 1e-30)
        scale[0:8] = m * (1.0 / 32767.0)
        inverse = 32767.0 / m

        def body(b, _):
            v = part[p, l, first + b].reshape(-1, 8, LANES) * inverse
            q[b] = jnp.round(v).astype(jnp.int32).astype(jnp.int16).reshape(2 * ROWS, LANES)
            return 0

        lax.fori_loop(0, count, body, 0)

    started = []

    def send(copies):
        for copy in copies:
            copy.start()
            started.append(copy)

    def z_copies(way, s, l):
        target = up if way == 0 else down
        return (
            remote(zsx.at[way, s, l], zrx.at[way, s, l], z_send.at[way, s, l, 0], z_recv.at[way, s, l, 0], target),
            remote(zs.at[way, s, l], zr.at[way, s, l], z_send.at[way, s, l, 1], z_recv.at[way, s, l, 1], target),
        )

    def x_copies(way, s):
        target = up if way == 0 else down
        if s == 0:
            blocks = pl.ds(0, XA) if way == 0 else pl.ds(XA, NX - XA)
        else:
            blocks = pl.ds(0, NX)
        return (
            remote(xsx.at[way, s], xrx.at[way, s], x_send.at[way, s, 0], x_recv.at[way, s, 0], target),
            remote(xs.at[way, s, blocks], xr.at[way, s, blocks], x_send.at[way, s, 1], x_recv.at[way, s, 1], target),
        )

    def e_copies(p):
        q, r = (es.at[p], er.at[p]) if p < 8 else (fs, fr)
        return (
            remote(esx.at[p], erx.at[p], e_send.at[p, 0], e_recv.at[p, 0], pair),
            remote(q, r, e_send.at[p, 1], e_recv.at[p, 1], pair),
        )

    def receive(copies):
        for copy in copies:
            copy.wait_recv()

    def z_receive(p, way, s, l):
        receive(z_copies(way, s, l))
        add(p, l, 0, NZ, zr.at[way, s, l], zrx.at[way, s, l])
        left[p, l] = left[p, l] + zrx[way, s, l, 8:16]

    def z_emit(p, way, s, l):
        quantize(p, l, 0, NZ, zs.at[way, s, l], zsx.at[way, s, l])
        zsx[way, s, l, 8:16] = left[p, l]
        send(z_copies(way, s, l))

    def x_receive(p, way, s):
        receive(x_copies(way, s))
        first, count = (0, NX) if s > 0 else ((0, XA) if way == 0 else (XA, NX - XA))
        add(p, xl, NZ + first, count, xr.at[way, s, pl.ds(first, count)], xrx.at[way, s])

    def x_emit(p, way, s):
        first, count = (0, NX) if s > 0 else ((0, XA) if way == 0 else (XA, NX - XA))
        quantize(p, xl, NZ + first, count, xs.at[way, s, pl.ds(first, count)], xsx.at[way, s])
        send(x_copies(way, s))

    def e_emit(p):
        quantize(p, 1 - xl, NZ, NX, es.at[p], esx.at[p])
        send(e_copies(p))

    def e_receive(p):
        receive(e_copies(p))
        add(p, xl, NZ, NX, er.at[p], erx.at[p])

    for p in (0, 1, 2):
        launch(p)
    arrive(0)
    launch(3)
    launch(4)
    arrive_sibling(0)
    b_copy.wait()
    multiply(0)
    e_emit(0)
    z_emit(0, 0, 0, 0)
    z_emit(0, 1, 0, 1)

    for s in (1, 2, 3, 4):
        now = (2 * s - 1, 2 * s) if s < 4 else (7,)
        for p in now:
            arrive(p)
        for p in (2 * s + 3, 2 * s + 4):
            if 4 < p < 8:
                launch(p)
        for p in now:
            arrive_sibling(p)
            multiply(p)
            e_emit(p)
        before = (2 * s - 3, 2 * s - 2) if s > 1 else (0, 0)
        if s == 1:
            e_receive(0)
            x_emit(0, 0, 0)
            x_emit(0, 1, 0)
        else:
            for way in (0, 1):
                p = before[way]
                e_receive(p)
                x_receive(p, way, s - 2)
                x_emit(p, way, s - 1)
        if s < 4:
            for way in (0, 1):
                p = now[way]
                for l in (way, 1 - way):
                    if s > 1 or l == way:
                        z_receive(p, way, s - 1, l)
                    z_emit(p, way, s, l)

    for way in (0, 1):
        z_receive(7, way, 3, 1 - xl)
    quantize(7, 1 - xl, 0, NZ, fs, esx.at[8])
    esx[8, 8:16] = left[7, 1 - xl]
    send(e_copies(8))
    for way in (0, 1):
        z_receive(7, way, 3, xl)
    e_receive(7)
    for way in (0, 1):
        x_receive(7, way, 3)

    def write(b):
        for side in range(2):
            out_ref[:, (2 * b + side) * LANES:(2 * b + side + 1) * LANES] = part[
                7, xl, b, side * ROWS:side * ROWS + rows]

    for b in range(NZ, NB):
        write(b)
    receive(e_copies(8))
    add(7, xl, 0, NZ, fr, erx.at[8])
    for b in range(NZ):
        write(b)
    tmp[0:8] = left[7, xl] + erx[8, 8:16]
    out_ref[:, NB * 256:] = tmp[...].T[0:rows, 0:tail]

    for p in range(8):
        for part_of in range(2):
            for when, copy in g_sends(p, part_of):
                if when is None:
                    copy.wait_send()
                else:
                    pl.when(when)(copy.wait_send)
    for copy in started:
        copy.wait_send()


def on_device(amplitudes, integrals, cd_blocks):
    rows, depth = amplitudes.shape
    width = integrals.shape[1]
    message = (2 * ROWS, LANES)
    dma = pltpu.SemaphoreType.DMA
    return pl.pallas_call(
        kernel,
        out_shape=jax.ShapeDtypeStruct((rows, width), F32),
        in_specs=[
            pl.BlockSpec(memory_space=pltpu.VMEM),
            pl.BlockSpec(memory_space=pltpu.SMEM),
            pl.BlockSpec(memory_space=pl.ANY),
        ],
        out_specs=pl.BlockSpec(memory_space=pltpu.VMEM),
        scratch_shapes=[
            pltpu.VMEM((8, 2, PAD, depth), jnp.bfloat16),
            pltpu.VMEM((depth, width), jnp.bfloat16),
            pltpu.VMEM((8, 2, NB) + message, F32),
            pltpu.VMEM((LANES, LANES), F32),
            pltpu.VMEM((8, 2, 8, LANES), F32),
            pltpu.VMEM((2, 4, 2, NZ) + message, jnp.int16),
            pltpu.VMEM((2, 4, 2, NZ) + message, jnp.int16),
            pltpu.VMEM((2, 4, 2, 16, LANES), F32),
            pltpu.VMEM((2, 4, 2, 16, LANES), F32),
            pltpu.VMEM((2, 4, NX) + message, jnp.int16),
            pltpu.VMEM((2, 4, NX) + message, jnp.int16),
            pltpu.VMEM((2, 4, 8, LANES), F32),
            pltpu.VMEM((2, 4, 8, LANES), F32),
            pltpu.VMEM((8, NX) + message, jnp.int16),
            pltpu.VMEM((8, NX) + message, jnp.int16),
            pltpu.VMEM((9, 16, LANES), F32),
            pltpu.VMEM((9, 16, LANES), F32),
            pltpu.VMEM((NZ,) + message, jnp.int16),
            pltpu.VMEM((NZ,) + message, jnp.int16),
            dma(()),
            dma((8, 2, 4)),
            dma((8, 2, 2)),
            dma((2, 4, 2, 2)),
            dma((2, 4, 2, 2)),
            dma((2, 4, 2)),
            dma((2, 4, 2)),
            dma((9, 2)),
            dma((9, 2)),
        ],
        compiler_params=pltpu.CompilerParams(
            collective_id=0, has_side_effects=True, vmem_limit_bytes=56 * 2**20
        ),
    )(amplitudes, cd_blocks, integrals)


def solution(mesh):
    return jax.shard_map(
        on_device,
        mesh=mesh,
        in_specs=(P("blk", "bulk"), P("bulk", "blk"), P("bulk", None)),
        out_specs=P("bulk", "blk"),
        check_vma=False,
    )
```

```python
import functools

import jax
import jax.numpy as jnp
from jax import lax
from jax.experimental import pallas as pl
from jax.experimental.pallas import tpu as pltpu
from jax.sharding import PartitionSpec as P

MESH = pl.DeviceIdType.MESH
F32 = jnp.float32

DELTA = (4, 3, 5, 2, 6, 1, 7, 0)
NZ = 2
NB = 7
NX = NB - NZ
XA = (NX + 1) // 2
LANES = 128
PAD = 112
ROWS = 104
FULL = 96
QUAD = 512
OWN, Y_M, Y_P, Y_2, R_OWN, R_M, R_P, R_2 = range(8)
LAST = 8
EARLY = (OWN, Y_M, Y_P)


def kernel(a_ref, cd_ref, b_hbm, out_ref, abuf, ebuf, b_ref, part, tmp, left, zs, zr, zsx, zrx, xs, xr, xsx, xrx,
           es, er, esx, erx, fs, fr, b_sem, g_send, g_recv, z_send, z_recv, x_send, x_recv, e_send, e_recv):
    rows, depth = a_ref.shape
    tail = b_hbm.shape[1] - 2 * NB * LANES
    blk, bulk = lax.axis_index("blk"), lax.axis_index("bulk")
    y, h, k = blk // 4, (blk // 2) % 2, blk % 2
    z, xl = bulk // 2, bulk % 2

    def at_y(step):
        return (((y + step + 4) % 4) * 4 + h * 2 + k, bulk)

    def at_z(step):
        return (blk, ((z + step + 8) % 8) * 2 + xl)

    up, down = at_z(1), at_z(-1)
    y_up, y_down = at_y(1), at_y(-1)
    across = (y * 4 + (1 - h) * 2 + k, bulk)
    sibling = (y * 4 + h * 2 + (1 - k), bulk)
    pair = (blk, z * 2 + (1 - xl))

    b_copy = pltpu.make_async_copy(b_hbm, b_ref, b_sem)
    b_copy.start()

    barrier = pltpu.get_barrier_semaphore()
    partners = (up, down, y_up, y_down, across, sibling, pair)
    for partner in partners:
        pl.semaphore_signal(barrier, inc=1, device_id=partner, device_id_type=MESH)

    def remote(src, dst, send, recv, target):
        return pltpu.make_async_remote_copy(
            src_ref=src, dst_ref=dst, send_sem=send, recv_sem=recv, device_id=target, device_id_type=MESH
        )

    def place(n):
        source = ((y + (0, -1, 1, 2)[n % 4] + 4) % 4) * 2 + (h if n < 4 else 1 - h)
        d = (source - z + 8) % 8
        return jnp.where(d < 4, 7 - 2 * d, 2 * (d - 4))

    places = [place(n) for n in range(8)]

    per_block = depth // cd_ref.shape[0]
    column = lax.broadcasted_iota(jnp.int32, (1, depth), 1)
    weight = jnp.zeros((1, depth), F32)
    for block in range(cd_ref.shape[0]):
        factor = jnp.where(cd_ref[block, 0] == cd_ref[block, 1], 1.0, 2.0).astype(F32)
        inside = jnp.logical_and(column >= block * per_block, column < (block + 1) * per_block)
        weight = jnp.where(inside, factor, weight)
    tmp[...] = jnp.zeros_like(tmp)
    weighted = a_ref[...].astype(F32) * weight
    main = 2 * NB * LANES
    abuf[OWN, k, 0:FULL, 0:main] = weighted[0:FULL, 0:main].astype(jnp.bfloat16)
    tmp[0:rows, 0:depth - main] = weighted[:, main:]
    ends = tmp[...].T[0:8]
    last = weighted[FULL:rows, 0:main]
    spare = jnp.concatenate([last[:, 3 * QUAD:], ends[0:4], ends[4:8]], axis=1)
    ebuf[OWN, k] = jnp.concatenate(
        [last[:, 0:QUAD], last[:, QUAD:2 * QUAD], last[:, 2 * QUAD:3 * QUAD], spare], axis=0).astype(jnp.bfloat16)
    tmp[...] = jnp.zeros_like(tmp)

    pl.semaphore_wait(barrier, len(partners))

    def half(n, l, part_of):
        if part_of == 2:
            return ebuf.at[n, l]
        return abuf.at[n, l, pl.ds(part_of * (FULL // 2), FULL // 2), pl.ds(0, main)]

    started = []

    def send(copies):
        for copy in copies:
            copy.start()
            started.append(copy)

    def give(source, target_slot, part_of, target):
        send([remote(half(source, k, part_of), half(target_slot, k, part_of), g_send.at[target_slot, part_of, 0],
                     g_recv.at[target_slot, k, part_of], target)])

    def share(n, part_of):
        ref = half(n, k, part_of)
        send([remote(ref, ref, g_send.at[n, part_of, 1], g_recv.at[n, k, part_of], sibling)])

    def arrive(n, part_of):
        ref = half(n, k, part_of)
        remote(ref, ref, g_send.at[n, part_of, 0], g_recv.at[n, k, part_of], sibling).wait_recv()
        share(n, part_of)

    def arrive_sibling(n):
        for part_of in range(3):
            ref = half(n, 1 - k, part_of)
            remote(ref, ref, g_send.at[n, part_of, 1], g_recv.at[n, 1 - k, part_of], sibling).wait_recv()

    def unpack(n):
        for l in range(2):
            e = ebuf[n, l].astype(F32)
            low = jnp.concatenate([e[0:4], e[4:8], e[8:12], e[12:16, 0:main - 3 * QUAD]], axis=1)
            low = jnp.concatenate([low, jnp.zeros((PAD - FULL - 4, main), F32)], axis=0)
            abuf[n, l, FULL:PAD, 0:main] = low.astype(jnp.bfloat16)
            ends = jnp.concatenate([e[12:16, QUAD - 2 * LANES:QUAD - LANES], e[12:16, QUAD - LANES:]], axis=0)
            abuf[n, l, :, main:] = ends.T[0:PAD].astype(jnp.bfloat16)

    def multiply(n, p):
        unpack(n)
        lhs = abuf[n].reshape(2 * PAD, depth)
        wide = NB * LANES

        def body(side, _):
            r = jnp.dot(lhs, b_ref[:, pl.ds(pl.multiple_of(side * wide, LANES), wide)], preferred_element_type=F32)
            for l in range(2):
                for b in range(NB):
                    part[p, l, b, pl.ds(pl.multiple_of(side * ROWS, 8), ROWS)] = r[
                        l * PAD:l * PAD + ROWS, b * LANES:(b + 1) * LANES]
            return 0

        lax.fori_loop(0, 2, body, 0)
        r = jnp.dot(lhs, b_ref[:, 2 * wide:], preferred_element_type=F32)
        for l in range(2):
            tmp[0:PAD, 0:tail] = r[l * PAD:(l + 1) * PAD]
            left[p, l] = tmp[...].T[0:8]

    def add(p, l, first, count, q, scale):
        factor = scale[0:8]

        def body(b, _):
            more = q[b].astype(F32).reshape(-1, 8, LANES) * factor
            v = part[p, l, first + b].reshape(-1, 8, LANES) + more
            part[p, l, first + b] = v.reshape(2 * ROWS, LANES)
            return 0

        lax.fori_loop(0, count, body, 0)

    def quantize(p, l, first, count, q, scale):
        def largest(b, m):
            v = jnp.abs(part[p, l, first + b].reshape(-1, 8, LANES))
            return jnp.maximum(m, jnp.max(v, axis=0))

        m = lax.fori_loop(0, count, largest, jnp.zeros((8, LANES), F32))
        m = jnp.maximum(m, 1e-30)
        scale[0:8] = m * (1.0 / 32767.0)
        inverse = 32767.0 / m

        def body(b, _):
            v = part[p, l, first + b].reshape(-1, 8, LANES) * inverse
            q[b] = jnp.round(v).astype(jnp.int32).astype(jnp.int16).reshape(2 * ROWS, LANES)
            return 0

        lax.fori_loop(0, count, body, 0)

    def z_copies(way, s, l):
        target = up if way == 0 else down
        return (
            remote(zsx.at[way, s, l], zrx.at[way, s, l], z_send.at[way, s, l, 0], z_recv.at[way, s, l, 0], target),
            remote(zs.at[way, s, l], zr.at[way, s, l], z_send.at[way, s, l, 1], z_recv.at[way, s, l, 1], target),
        )

    def x_copies(way, s):
        target = up if way == 0 else down
        if s == 0:
            blocks = pl.ds(0, XA) if way == 0 else pl.ds(XA, NX - XA)
        else:
            blocks = pl.ds(0, NX)
        return (
            remote(xsx.at[way, s], xrx.at[way, s], x_send.at[way, s, 0], x_recv.at[way, s, 0], target),
            remote(xs.at[way, s, blocks], xr.at[way, s, blocks], x_send.at[way, s, 1], x_recv.at[way, s, 1], target),
        )

    def e_copies(p):
        q, r = (fs, fr) if p is LAST else (es.at[p], er.at[p])
        return (
            remote(esx.at[p], erx.at[p], e_send.at[p, 0], e_recv.at[p, 0], pair),
            remote(q, r, e_send.at[p, 1], e_recv.at[p, 1], pair),
        )

    def receive(copies):
        for copy in copies:
            copy.wait_recv()

    def z_receive(p, way, s, l):
        receive(z_copies(way, s, l))
        add(p, l, 0, NZ, zr.at[way, s, l], zrx.at[way, s, l])
        left[p, l] = left[p, l] + zrx[way, s, l, 8:16]

    def z_emit(p, way, s, l):
        quantize(p, l, 0, NZ, zs.at[way, s, l], zsx.at[way, s, l])
        zsx[way, s, l, 8:16] = left[p, l]
        send(z_copies(way, s, l))

    def x_receive(p, way, s):
        receive(x_copies(way, s))
        first, count = (0, NX) if s > 0 else ((0, XA) if way == 0 else (XA, NX - XA))
        add(p, xl, NZ + first, count, xr.at[way, s, pl.ds(first, count)], xrx.at[way, s])

    def x_emit(p, way, s):
        first, count = (0, NX) if s > 0 else ((0, XA) if way == 0 else (XA, NX - XA))
        quantize(p, xl, NZ + first, count, xs.at[way, s, pl.ds(first, count)], xsx.at[way, s])
        send(x_copies(way, s))

    def e_emit(p):
        quantize(p, 1 - xl, NZ, NX, es.at[p], esx.at[p])
        send(e_copies(p))

    def e_receive(p):
        receive(e_copies(p))
        add(p, xl, NZ, NX, er.at[p], erx.at[p])

    for part_of in range(3):
        give(OWN, Y_M, part_of, y_up)
        give(OWN, Y_P, part_of, y_down)
        give(OWN, R_OWN, part_of, across)
        share(OWN, part_of)
    b_copy.wait()
    arrive_sibling(OWN)
    multiply(OWN, places[OWN])
    arrive(Y_M, 0)
    give(Y_M, Y_2, 0, y_up)
    arrive(Y_P, 0)
    arrive(R_OWN, 0)
    give(R_OWN, R_M, 0, y_up)
    give(R_OWN, R_P, 0, y_down)
    for part_of in (1, 2):
        arrive(Y_P, part_of)
        give(Y_P, Y_2, part_of, y_down)
    for part_of in (1, 2):
        arrive(R_OWN, part_of)
        give(R_OWN, R_M, part_of, y_up)
        give(R_OWN, R_P, part_of, y_down)
    for part_of in (1, 2):
        arrive(Y_M, part_of)
    e_emit(places[OWN])
    for n in (Y_M, Y_P):
        arrive_sibling(n)
        multiply(n, places[n])
    for part_of in range(3):
        arrive(Y_2, part_of)
        give(Y_2, R_2, part_of, across)
    e_emit(places[Y_M])
    e_emit(places[Y_P])
    for n in (R_OWN, Y_2):
        arrive_sibling(n)
        multiply(n, places[n])
    for n in (R_M, R_P, R_2):
        for part_of in range(3):
            arrive(n, part_of)
    for n in (R_M, R_P, R_2):
        arrive_sibling(n)
    keys = [places[n] * 8 + n for n in (R_M, R_P, R_2)]
    low, high = jnp.minimum(keys[0], keys[1]), jnp.maximum(keys[0], keys[1])
    first, second = jnp.minimum(low, keys[2]), jnp.maximum(low, jnp.minimum(high, keys[2]))
    third = jnp.maximum(high, keys[2])

    def e_late(p):
        early = [places[n] == p for n in EARLY]
        done = functools.reduce(jnp.logical_or, early)

        @pl.when(jnp.logical_not(done))
        def _():
            quantize(p, 1 - xl, NZ, NX, es.at[p], esx.at[p])
            for copy in e_copies(p):
                copy.start()

        late.append((done, p))

    late = []
    chunks = ((0, 0), (1, 2), (3, 4), (5, 6))

    def z_part(s, way, l):
        p = chunks[s][way]
        if s > 1 or (s == 1 and l == way):
            z_receive(p, way, s - 1, l)
        z_emit(p, way, s, l)

    def x_step(s):
        if s == 0:
            e_receive(0)
        for way in (0, 1):
            p = chunks[s][way]
            if s > 0:
                e_receive(p)
                x_receive(p, way, s - 1)
            x_emit(p, way, s)

    multiply(first % 8, first // 8)
    e_late(0)
    z_part(0, 0, 0)
    z_part(0, 1, 1)
    multiply(second % 8, second // 8)
    z_part(1, 0, 1)
    multiply(third % 8, third // 8)
    z_part(1, 1, 0)
    for p in range(1, 8):
        e_late(p)
    z_part(1, 0, 0)
    z_part(1, 1, 1)
    x_step(0)
    for s in (2, 3):
        for l in range(2):
            for way in (0, 1):
                z_part(s, way, l)
        x_step(s - 1)
    x_step(3)

    for way in (0, 1):
        z_receive(7, way, 3, 1 - xl)
    quantize(7, 1 - xl, 0, NZ, fs, esx.at[LAST])
    esx[LAST, 8:16] = left[7, 1 - xl]
    send(e_copies(LAST))
    for way in (0, 1):
        z_receive(7, way, 3, xl)
    e_receive(7)
    for way in (0, 1):
        x_receive(7, way, 3)

    def write(b):
        for side in range(2):
            first = (side * NB + b) * LANES
            out_ref[:, first:first + LANES] = part[7, xl, b, side * ROWS:side * ROWS + rows]

    for b in range(NZ, NB):
        write(b)
    receive(e_copies(LAST))
    add(7, xl, 0, NZ, fr, erx.at[LAST])
    for b in range(NZ):
        write(b)
    tmp[0:8] = left[7, xl] + erx[LAST, 8:16]
    out_ref[:, 2 * NB * LANES:] = tmp[...].T[0:rows, 0:tail]

    for done, p in late:
        @pl.when(jnp.logical_not(done))
        def _(p=p):
            for copy in e_copies(p):
                copy.wait_send()
    for copy in started:
        copy.wait_send()


def on_device(amplitudes, integrals, cd_blocks):
    rows, depth = amplitudes.shape
    width = integrals.shape[1]
    message = (2 * ROWS, LANES)
    dma = pltpu.SemaphoreType.DMA
    return pl.pallas_call(
        kernel,
        out_shape=jax.ShapeDtypeStruct((rows, width), F32),
        in_specs=[
            pl.BlockSpec(memory_space=pltpu.VMEM),
            pl.BlockSpec(memory_space=pltpu.SMEM),
            pl.BlockSpec(memory_space=pl.ANY),
        ],
        out_specs=pl.BlockSpec(memory_space=pltpu.VMEM),
        scratch_shapes=[
            pltpu.VMEM((8, 2, PAD, depth), jnp.bfloat16),
            pltpu.VMEM((8, 2, 16, QUAD), jnp.bfloat16),
            pltpu.VMEM((depth, width), jnp.bfloat16),
            pltpu.VMEM((8, 2, NB) + message, F32),
            pltpu.VMEM((LANES, LANES), F32),
            pltpu.VMEM((8, 2, 8, LANES), F32),
            pltpu.VMEM((2, 4, 2, NZ) + message, jnp.int16),
            pltpu.VMEM((2, 4, 2, NZ) + message, jnp.int16),
            pltpu.VMEM((2, 4, 2, 16, LANES), F32),
            pltpu.VMEM((2, 4, 2, 16, LANES), F32),
            pltpu.VMEM((2, 4, NX) + message, jnp.int16),
            pltpu.VMEM((2, 4, NX) + message, jnp.int16),
            pltpu.VMEM((2, 4, 8, LANES), F32),
            pltpu.VMEM((2, 4, 8, LANES), F32),
            pltpu.VMEM((8, NX) + message, jnp.int16),
            pltpu.VMEM((8, NX) + message, jnp.int16),
            pltpu.VMEM((9, 16, LANES), F32),
            pltpu.VMEM((9, 16, LANES), F32),
            pltpu.VMEM((NZ,) + message, jnp.int16),
            pltpu.VMEM((NZ,) + message, jnp.int16),
            dma(()),
            dma((8, 3, 2)),
            dma((8, 2, 3)),
            dma((2, 4, 2, 2)),
            dma((2, 4, 2, 2)),
            dma((2, 4, 2)),
            dma((2, 4, 2)),
            dma((9, 2)),
            dma((9, 2)),
        ],
        compiler_params=pltpu.CompilerParams(
            collective_id=0, has_side_effects=True, vmem_limit_bytes=56 * 2**20
        ),
    )(amplitudes, cd_blocks, integrals)


def solution(mesh):
    return jax.shard_map(
        on_device,
        mesh=mesh,
        in_specs=(P("blk", "bulk"), P("bulk", "blk"), P("bulk", None)),
        out_specs=P("bulk", "blk"),
        check_vma=False,
    )
```

```python
import functools

import jax
import jax.numpy as jnp
from jax import lax
from jax.experimental import pallas as pl
from jax.experimental.pallas import tpu as pltpu
from jax.sharding import PartitionSpec as P

MESH = pl.DeviceIdType.MESH
F32 = jnp.float32

DELTA = (4, 3, 5, 2, 6, 1, 7, 0)
NZ = 3
NB = 7
NX = NB - NZ
XA = (NX + 1) // 2
LANES = 128
PAD = 112
ROWS = 104
FULL = 96
QUAD = 512
OWN, Y_M, Y_P, Y_2, R_OWN, R_M, R_P, R_2 = range(8)
LAST = 8
EARLY = (OWN, Y_M, Y_P, R_OWN, Y_2)


def kernel(a_ref, cd_ref, b_hbm, out_ref, abuf, ebuf, b_ref, part, tmp, left, zs, zr, zsx, zrx, xs, xr, xsx, xrx,
           es, er, esx, erx, fs, fr, b_sem, g_send, g_recv, z_send, z_recv, x_send, x_recv, e_send, e_recv):
    rows, depth = a_ref.shape
    tail = b_hbm.shape[1] - 2 * NB * LANES
    blk, bulk = lax.axis_index("blk"), lax.axis_index("bulk")
    y, h, k = blk // 4, (blk // 2) % 2, blk % 2
    z, xl = bulk // 2, bulk % 2

    def at_y(step):
        return (((y + step + 4) % 4) * 4 + h * 2 + k, bulk)

    def at_z(step):
        return (blk, ((z + step + 8) % 8) * 2 + xl)

    up, down = at_z(1), at_z(-1)
    y_up, y_down = at_y(1), at_y(-1)
    across = (y * 4 + (1 - h) * 2 + k, bulk)
    sibling = (y * 4 + h * 2 + (1 - k), bulk)
    pair = (blk, z * 2 + (1 - xl))

    b_copy = pltpu.make_async_copy(b_hbm, b_ref, b_sem)
    b_copy.start()

    barrier = pltpu.get_barrier_semaphore()
    partners = (up, down, y_up, y_down, across, sibling, pair)
    for partner in partners:
        pl.semaphore_signal(barrier, inc=1, device_id=partner, device_id_type=MESH)

    def remote(src, dst, send, recv, target):
        return pltpu.make_async_remote_copy(
            src_ref=src, dst_ref=dst, send_sem=send, recv_sem=recv, device_id=target, device_id_type=MESH
        )

    def place(n):
        source = ((y + (0, -1, 1, 2)[n % 4] + 4) % 4) * 2 + (h if n < 4 else 1 - h)
        d = (source - z + 8) % 8
        return jnp.where(d < 4, 7 - 2 * d, 2 * (d - 4))

    places = [place(n) for n in range(8)]

    per_block = depth // cd_ref.shape[0]
    column = lax.broadcasted_iota(jnp.int32, (1, depth), 1)
    weight = jnp.zeros((1, depth), F32)
    for block in range(cd_ref.shape[0]):
        factor = jnp.where(cd_ref[block, 0] == cd_ref[block, 1], 1.0, 2.0).astype(F32)
        inside = jnp.logical_and(column >= block * per_block, column < (block + 1) * per_block)
        weight = jnp.where(inside, factor, weight)
    tmp[...] = jnp.zeros_like(tmp)
    weighted = a_ref[...].astype(F32) * weight
    main = 2 * NB * LANES
    abuf[OWN, k, 0:FULL, 0:main] = weighted[0:FULL, 0:main].astype(jnp.bfloat16)
    tmp[0:rows, 0:depth - main] = weighted[:, main:]
    ends = tmp[...].T[0:8]
    last = weighted[FULL:rows, 0:main]
    spare = jnp.concatenate([last[:, 3 * QUAD:], ends[0:4], ends[4:8]], axis=1)
    ebuf[OWN, k] = jnp.concatenate(
        [last[:, 0:QUAD], last[:, QUAD:2 * QUAD], last[:, 2 * QUAD:3 * QUAD], spare], axis=0).astype(jnp.bfloat16)
    tmp[...] = jnp.zeros_like(tmp)

    pl.semaphore_wait(barrier, len(partners))

    def half(n, l, part_of):
        if part_of == 2:
            return ebuf.at[n, l]
        return abuf.at[n, l, pl.ds(part_of * (FULL // 2), FULL // 2), pl.ds(0, main)]

    started = []

    def send(copies):
        for copy in copies:
            copy.start()
            started.append(copy)

    def give(source, target_slot, part_of, target):
        send([remote(half(source, k, part_of), half(target_slot, k, part_of), g_send.at[target_slot, part_of, 0],
                     g_recv.at[target_slot, k, part_of], target)])

    def share(n, part_of):
        ref = half(n, k, part_of)
        send([remote(ref, ref, g_send.at[n, part_of, 1], g_recv.at[n, k, part_of], sibling)])

    def arrive(n, part_of):
        ref = half(n, k, part_of)
        remote(ref, ref, g_send.at[n, part_of, 0], g_recv.at[n, k, part_of], sibling).wait_recv()
        share(n, part_of)

    def arrive_sibling(n):
        for part_of in range(3):
            ref = half(n, 1 - k, part_of)
            remote(ref, ref, g_send.at[n, part_of, 1], g_recv.at[n, 1 - k, part_of], sibling).wait_recv()

    def unpack(n):
        for l in range(2):
            e = ebuf[n, l].astype(F32)
            low = jnp.concatenate([e[0:4], e[4:8], e[8:12], e[12:16, 0:main - 3 * QUAD]], axis=1)
            low = jnp.concatenate([low, jnp.zeros((PAD - FULL - 4, main), F32)], axis=0)
            abuf[n, l, FULL:PAD, 0:main] = low.astype(jnp.bfloat16)
            ends = jnp.concatenate([e[12:16, QUAD - 2 * LANES:QUAD - LANES], e[12:16, QUAD - LANES:]], axis=0)
            abuf[n, l, :, main:] = ends.T[0:PAD].astype(jnp.bfloat16)

    def multiply(n, p, sides=(0, 2)):
        lhs = abuf[n].reshape(2 * PAD, depth)
        wide = NB * LANES

        def body(side, _):
            r = jnp.dot(lhs, b_ref[:, pl.ds(pl.multiple_of(side * wide, LANES), wide)], preferred_element_type=F32)
            for l in range(2):
                for j in range(NB):
                    tile = side * NB + j
                    part[p, l, tile // 2, pl.ds(pl.multiple_of(tile % 2 * ROWS, 8), ROWS)] = r[
                        l * PAD:l * PAD + ROWS, j * LANES:(j + 1) * LANES]
            return 0

        lax.fori_loop(sides[0], sides[1], body, 0)

    def prepare(n, p):
        unpack(n)
        r = jnp.dot(abuf[n].reshape(2 * PAD, depth), b_ref[:, main:], preferred_element_type=F32)
        for l in range(2):
            tmp[0:PAD, 0:tail] = r[l * PAD:(l + 1) * PAD]
            left[p, l] = tmp[...].T[0:8]

    def add(p, l, first, count, q, scale):
        factor = scale[0:8]

        def body(b, _):
            more = q[b].astype(F32).reshape(-1, 8, LANES) * factor
            v = part[p, l, first + b].reshape(-1, 8, LANES) + more
            part[p, l, first + b] = v.reshape(2 * ROWS, LANES)
            return 0

        lax.fori_loop(0, count, body, 0)

    def quantize(p, l, first, count, q, scale):
        def largest(b, m):
            v = jnp.abs(part[p, l, first + b].reshape(-1, 8, LANES))
            return jnp.maximum(m, jnp.max(v, axis=0))

        m = lax.fori_loop(0, count, largest, jnp.zeros((8, LANES), F32))
        m = jnp.maximum(m, 1e-30)
        scale[0:8] = m * (1.0 / 32767.0)
        inverse = 32767.0 / m

        def body(b, _):
            v = part[p, l, first + b].reshape(-1, 8, LANES) * inverse
            q[b] = jnp.round(v).astype(jnp.int32).astype(jnp.int16).reshape(2 * ROWS, LANES)
            return 0

        lax.fori_loop(0, count, body, 0)

    def z_copies(way, s, l):
        target = up if way == 0 else down
        return (
            remote(zsx.at[way, s, l], zrx.at[way, s, l], z_send.at[way, s, l, 0], z_recv.at[way, s, l, 0], target),
            remote(zs.at[way, s, l], zr.at[way, s, l], z_send.at[way, s, l, 1], z_recv.at[way, s, l, 1], target),
        )

    def x_copies(way, s):
        target = up if way == 0 else down
        if s == 0:
            blocks = pl.ds(0, XA) if way == 0 else pl.ds(XA, NX - XA)
        else:
            blocks = pl.ds(0, NX)
        return (
            remote(xsx.at[way, s], xrx.at[way, s], x_send.at[way, s, 0], x_recv.at[way, s, 0], target),
            remote(xs.at[way, s, blocks], xr.at[way, s, blocks], x_send.at[way, s, 1], x_recv.at[way, s, 1], target),
        )

    def e_copies(p):
        q, r = (fs, fr) if p is LAST else (es.at[p], er.at[p])
        return (
            remote(esx.at[p], erx.at[p], e_send.at[p, 0], e_recv.at[p, 0], pair),
            remote(q, r, e_send.at[p, 1], e_recv.at[p, 1], pair),
        )

    def receive(copies):
        for copy in copies:
            copy.wait_recv()

    def z_receive(p, way, s, l):
        receive(z_copies(way, s, l))
        add(p, l, 0, NZ, zr.at[way, s, l], zrx.at[way, s, l])
        left[p, l] = left[p, l] + zrx[way, s, l, 8:16]

    def x_receive(p, way, s):
        receive(x_copies(way, s))
        first, count = (0, NX) if s > 0 else ((0, XA) if way == 0 else (XA, NX - XA))
        add(p, xl, NZ + first, count, xr.at[way, s, pl.ds(first, count)], xrx.at[way, s])

    def x_emit(p, way, s):
        first, count = (0, NX) if s > 0 else ((0, XA) if way == 0 else (XA, NX - XA))
        quantize(p, xl, NZ + first, count, xs.at[way, s, pl.ds(first, count)], xsx.at[way, s])
        send(x_copies(way, s))

    def e_emit(p):
        quantize(p, 1 - xl, NZ, NX, es.at[p], esx.at[p])
        send(e_copies(p))

    def e_receive(p):
        receive(e_copies(p))
        add(p, xl, NZ, NX, er.at[p], erx.at[p])

    chunks = ((0, 0), (1, 2), (3, 4), (5, 6))


    def z_part(s, way, l):
        p = chunks[s][way]

        if s > 1 or (s == 1 and l == way):
            z_receive(p, way, s - 1, l)
        quantize(p, l, 0, NZ, zs.at[way, s, l], zsx.at[way, s, l])
        zsx[way, s, l, 8:16] = left[p, l]
        for copy in z_copies(way, s, l):
            copy.start()

    def give_all(source, slot, order, target):
        for part_of in order:
            give(source, slot, part_of, target)

    rising, falling = (0, 1, 2), (2, 1, 0)
    for i in range(3):
        give(OWN, Y_M, rising[i], y_up)
        give(OWN, Y_P, falling[i], y_down)
        give(OWN, R_OWN, rising[i], across)
    for part_of in range(3):
        share(OWN, part_of)
    b_copy.wait()
    arrive_sibling(OWN)
    prepare(OWN, places[OWN])
    multiply(OWN, places[OWN])
    e_emit(places[OWN])
    arrive(Y_M, 0)
    give(Y_M, Y_2, 0, y_up)
    for part_of in (2, 1):
        arrive(Y_P, part_of)
        give(Y_P, Y_2, part_of, y_down)
    arrive(R_OWN, 0)
    give(R_OWN, R_M, 0, y_up)
    for part_of in (2, 1):
        arrive(R_OWN, part_of)
        give(R_OWN, R_P, part_of, y_down)
    give_all(R_OWN, R_M, (1, 2), y_up)
    give(R_OWN, R_P, 0, y_down)
    for part_of in (1, 2):
        arrive(Y_M, part_of)
    arrive(Y_P, 0)
    arrive_sibling(Y_M)
    prepare(Y_M, places[Y_M])
    multiply(Y_M, places[Y_M])
    for part_of in range(3):
        arrive(Y_2, part_of)
    e_emit(places[Y_M])
    arrive_sibling(Y_P)
    prepare(Y_P, places[Y_P])
    multiply(Y_P, places[Y_P])
    arrive(R_M, 0)
    give(R_M, R_2, 0, y_up)
    for part_of in (2, 1):
        arrive(R_P, part_of)
        give(R_P, R_2, part_of, y_down)
    e_emit(places[Y_P])
    arrive_sibling(R_OWN)
    prepare(R_OWN, places[R_OWN])
    multiply(R_OWN, places[R_OWN])
    e_emit(places[R_OWN])
    for part_of in (1, 2):
        arrive(R_M, part_of)
    arrive(R_P, 0)
    arrive_sibling(Y_2)
    prepare(Y_2, places[Y_2])
    multiply(Y_2, places[Y_2])
    e_emit(places[Y_2])
    arrive_sibling(R_M)
    prepare(R_M, places[R_M])
    multiply(R_M, places[R_M])
    for part_of in range(3):
        arrive(R_2, part_of)
    arrive_sibling(R_P)
    arrive_sibling(R_2)
    keys = [places[n] * 8 + n for n in (R_P, R_2)]
    first, second = jnp.minimum(keys[0], keys[1]), jnp.maximum(keys[0], keys[1])

    def e_late(p):
        early = [places[n] == p for n in EARLY]
        done = functools.reduce(jnp.logical_or, early)

        @pl.when(jnp.logical_not(done))
        def _():
            quantize(p, 1 - xl, NZ, NX, es.at[p], esx.at[p])
            for copy in e_copies(p):
                copy.start()

        late.append((done, p))

    late = []

    def x_step(s):
        if s == 0:
            e_receive(0)
        for way in (0, 1):
            p = chunks[s][way]
            if s > 0:
                e_receive(p)
                x_receive(p, way, s - 1)
            x_emit(p, way, s)

    prepare(first % 8, first // 8)
    multiply(first % 8, first // 8, (0, 1))
    z_part(0, 0, 0)
    z_part(0, 1, 1)
    multiply(first % 8, first // 8, (1, 2))
    e_late(0)
    prepare(second % 8, second // 8)
    multiply(second % 8, second // 8, (0, 1))
    z_part(1, 0, 1)
    z_part(1, 1, 0)
    multiply(second % 8, second // 8, (1, 2))
    for p in range(1, 8):
        e_late(p)
    z_part(1, 0, 0)
    z_part(1, 1, 1)
    x_step(0)
    for l in (0, 1):
        for way in (0, 1):
            z_part(2, way, l)
    x_step(1)
    for way in (0, 1):
        z_part(3, way, 1 - xl)
    x_step(2)
    for way in (0, 1):
        z_part(3, way, xl)
    x_step(3)

    for way in (0, 1):
        z_receive(7, way, 3, 1 - xl)
    quantize(7, 1 - xl, 0, NZ, fs, esx.at[LAST])
    esx[LAST, 8:16] = left[7, 1 - xl]
    send(e_copies(LAST))
    for way in (0, 1):
        z_receive(7, way, 3, xl)
    e_receive(7)
    for way in (0, 1):
        x_receive(7, way, 3)

    def write(b):
        for side in range(2):
            first = (2 * b + side) * LANES
            out_ref[:, first:first + LANES] = part[7, xl, b, side * ROWS:side * ROWS + rows]

    for b in range(NZ, NB):
        write(b)
    receive(e_copies(LAST))
    add(7, xl, 0, NZ, fr, erx.at[LAST])
    for b in range(NZ):
        write(b)
    tmp[0:8] = left[7, xl] + erx[LAST, 8:16]
    out_ref[:, 2 * NB * LANES:] = tmp[...].T[0:rows, 0:tail]

    for done, p in late:
        @pl.when(jnp.logical_not(done))
        def _(p=p):
            for copy in e_copies(p):
                copy.wait_send()
    for s in range(4):
        for way in (0, 1):
            for l in (0, 1) if s > 0 else (way,):
                for copy in z_copies(way, s, l):
                    copy.wait_send()
    for copy in started:
        copy.wait_send()


def on_device(amplitudes, integrals, cd_blocks):
    rows, depth = amplitudes.shape
    width = integrals.shape[1]
    message = (2 * ROWS, LANES)
    dma = pltpu.SemaphoreType.DMA
    return pl.pallas_call(
        kernel,
        out_shape=jax.ShapeDtypeStruct((rows, width), F32),
        in_specs=[
            pl.BlockSpec(memory_space=pltpu.VMEM),
            pl.BlockSpec(memory_space=pltpu.SMEM),
            pl.BlockSpec(memory_space=pl.ANY),
        ],
        out_specs=pl.BlockSpec(memory_space=pltpu.VMEM),
        scratch_shapes=[
            pltpu.VMEM((8, 2, PAD, depth), jnp.bfloat16),
            pltpu.VMEM((8, 2, 16, QUAD), jnp.bfloat16),
            pltpu.VMEM((depth, width), jnp.bfloat16),
            pltpu.VMEM((8, 2, NB) + message, F32),
            pltpu.VMEM((LANES, LANES), F32),
            pltpu.VMEM((8, 2, 8, LANES), F32),
            pltpu.VMEM((2, 4, 2, NZ) + message, jnp.int16),
            pltpu.VMEM((2, 4, 2, NZ) + message, jnp.int16),
            pltpu.VMEM((2, 4, 2, 16, LANES), F32),
            pltpu.VMEM((2, 4, 2, 16, LANES), F32),
            pltpu.VMEM((2, 4, NX) + message, jnp.int16),
            pltpu.VMEM((2, 4, NX) + message, jnp.int16),
            pltpu.VMEM((2, 4, 8, LANES), F32),
            pltpu.VMEM((2, 4, 8, LANES), F32),
            pltpu.VMEM((8, NX) + message, jnp.int16),
            pltpu.VMEM((8, NX) + message, jnp.int16),
            pltpu.VMEM((9, 16, LANES), F32),
            pltpu.VMEM((9, 16, LANES), F32),
            pltpu.VMEM((NZ,) + message, jnp.int16),
            pltpu.VMEM((NZ,) + message, jnp.int16),
            dma(()),
            dma((8, 3, 2)),
            dma((8, 2, 3)),
            dma((2, 4, 2, 2)),
            dma((2, 4, 2, 2)),
            dma((2, 4, 2)),
            dma((2, 4, 2)),
            dma((9, 2)),
            dma((9, 2)),
        ],
        compiler_params=pltpu.CompilerParams(
            collective_id=0, has_side_effects=True, vmem_limit_bytes=56 * 2**20
        ),
    )(amplitudes, cd_blocks, integrals)


def solution(mesh):
    return jax.shard_map(
        on_device,
        mesh=mesh,
        in_specs=(P("blk", "bulk"), P("bulk", "blk"), P("bulk", None)),
        out_specs=P("bulk", "blk"),
        check_vma=False,
    )
```

```python
import functools

import jax
import jax.numpy as jnp
from jax import lax
from jax.experimental import pallas as pl
from jax.experimental.pallas import tpu as pltpu
from jax.sharding import PartitionSpec as P

MESH = pl.DeviceIdType.MESH
F32 = jnp.float32

DELTA = (4, 3, 5, 2, 6, 1, 7, 0)
NZ = 3
NB = 7
NX = NB - NZ
XA = (NX + 1) // 2
LANES = 128
PAD = 112
ROWS = 104
FULL = 96
QUAD = 512
OWN, Y_M, Y_P, Y_2, R_OWN, R_M, R_P, R_2 = range(8)
LAST = 8
EARLY = (OWN, Y_M, Y_P)


def kernel(a_ref, cd_ref, b_hbm, out_ref, abuf, ebuf, b_ref, part, tmp, left, zs, zr, zsx, zrx, xs, xr, xsx, xrx,
           es, er, esx, erx, fs, fr, b_sem, g_send, g_recv, z_send, z_recv, x_send, x_recv, e_send, e_recv):
    rows, depth = a_ref.shape
    tail = b_hbm.shape[1] - 2 * NB * LANES
    blk, bulk = lax.axis_index("blk"), lax.axis_index("bulk")
    y, h, k = blk // 4, (blk // 2) % 2, blk % 2
    z, xl = bulk // 2, bulk % 2

    def at_y(step):
        return (((y + step + 4) % 4) * 4 + h * 2 + k, bulk)

    def at_z(step):
        return (blk, ((z + step + 8) % 8) * 2 + xl)

    up, down = at_z(1), at_z(-1)
    y_up, y_down = at_y(1), at_y(-1)
    across = (y * 4 + (1 - h) * 2 + k, bulk)
    sibling = (y * 4 + h * 2 + (1 - k), bulk)
    pair = (blk, z * 2 + (1 - xl))

    b_copy = pltpu.make_async_copy(b_hbm, b_ref, b_sem)
    b_copy.start()

    barrier = pltpu.get_barrier_semaphore()
    partners = (up, down, y_up, y_down, across, sibling, pair)
    for partner in partners:
        pl.semaphore_signal(barrier, inc=1, device_id=partner, device_id_type=MESH)

    def remote(src, dst, send, recv, target):
        return pltpu.make_async_remote_copy(
            src_ref=src, dst_ref=dst, send_sem=send, recv_sem=recv, device_id=target, device_id_type=MESH
        )

    def place(n):
        source = ((y + (0, -1, 1, 2)[n % 4] + 4) % 4) * 2 + (h if n < 4 else 1 - h)
        d = (source - z + 8) % 8
        return jnp.where(d < 4, 7 - 2 * d, 2 * (d - 4))

    places = [place(n) for n in range(8)]

    per_block = depth // cd_ref.shape[0]
    column = lax.broadcasted_iota(jnp.int32, (1, depth), 1)
    weight = jnp.zeros((1, depth), F32)
    for block in range(cd_ref.shape[0]):
        factor = jnp.where(cd_ref[block, 0] == cd_ref[block, 1], 1.0, 2.0).astype(F32)
        inside = jnp.logical_and(column >= block * per_block, column < (block + 1) * per_block)
        weight = jnp.where(inside, factor, weight)
    tmp[...] = jnp.zeros_like(tmp)
    weighted = a_ref[...].astype(F32) * weight
    main = 2 * NB * LANES
    abuf[OWN, k, 0:FULL, 0:main] = weighted[0:FULL, 0:main].astype(jnp.bfloat16)
    tmp[0:rows, 0:depth - main] = weighted[:, main:]
    ends = tmp[...].T[0:8]
    last = weighted[FULL:rows, 0:main]
    spare = jnp.concatenate([last[:, 3 * QUAD:], ends[0:4], ends[4:8]], axis=1)
    ebuf[OWN, k] = jnp.concatenate(
        [last[:, 0:QUAD], last[:, QUAD:2 * QUAD], last[:, 2 * QUAD:3 * QUAD], spare], axis=0).astype(jnp.bfloat16)
    tmp[...] = jnp.zeros_like(tmp)

    pl.semaphore_wait(barrier, len(partners))

    def half(n, l, part_of):
        if part_of == 2:
            return ebuf.at[n, l]
        return abuf.at[n, l, pl.ds(part_of * (FULL // 2), FULL // 2), pl.ds(0, main)]

    started = []

    def send(copies):
        for copy in copies:
            copy.start()
            started.append(copy)

    def give(source, target_slot, part_of, target):
        send([remote(half(source, k, part_of), half(target_slot, k, part_of), g_send.at[target_slot, part_of, 0],
                     g_recv.at[target_slot, k, part_of], target)])

    def share(n, part_of):
        ref = half(n, k, part_of)
        send([remote(ref, ref, g_send.at[n, part_of, 1], g_recv.at[n, k, part_of], sibling)])

    def arrive(n, part_of):
        ref = half(n, k, part_of)
        remote(ref, ref, g_send.at[n, part_of, 0], g_recv.at[n, k, part_of], sibling).wait_recv()
        share(n, part_of)

    def arrive_sibling(n):
        for part_of in range(3):
            ref = half(n, 1 - k, part_of)
            remote(ref, ref, g_send.at[n, part_of, 1], g_recv.at[n, 1 - k, part_of], sibling).wait_recv()

    def unpack(n):
        for l in range(2):
            e = ebuf[n, l].astype(F32)
            low = jnp.concatenate([e[0:4], e[4:8], e[8:12], e[12:16, 0:main - 3 * QUAD]], axis=1)
            low = jnp.concatenate([low, jnp.zeros((PAD - FULL - 4, main), F32)], axis=0)
            abuf[n, l, FULL:PAD, 0:main] = low.astype(jnp.bfloat16)
            ends = jnp.concatenate([e[12:16, QUAD - 2 * LANES:QUAD - LANES], e[12:16, QUAD - LANES:]], axis=0)
            abuf[n, l, :, main:] = ends.T[0:PAD].astype(jnp.bfloat16)

    def multiply(n, p, sides=(0, 2)):
        lhs = abuf[n].reshape(2 * PAD, depth)
        wide = NB * LANES

        def body(side, _):
            r = jnp.dot(lhs, b_ref[:, pl.ds(pl.multiple_of(side * wide, LANES), wide)], preferred_element_type=F32)
            for l in range(2):
                for j in range(NB):
                    tile = side * NB + j
                    part[p, l, tile // 2, pl.ds(pl.multiple_of(tile % 2 * ROWS, 8), ROWS)] = r[
                        l * PAD:l * PAD + ROWS, j * LANES:(j + 1) * LANES]
            return 0

        lax.fori_loop(sides[0], sides[1], body, 0)

    def prepare(n, p):
        unpack(n)
        r = jnp.dot(abuf[n].reshape(2 * PAD, depth), b_ref[:, main:], preferred_element_type=F32)
        for l in range(2):
            tmp[0:PAD, 0:tail] = r[l * PAD:(l + 1) * PAD]
            left[p, l] = tmp[...].T[0:8]

    def add(p, l, first, count, q, scale):
        factor = scale[0:8]

        def body(b, _):
            more = q[b].astype(F32).reshape(-1, 8, LANES) * factor
            v = part[p, l, first + b].reshape(-1, 8, LANES) + more
            part[p, l, first + b] = v.reshape(2 * ROWS, LANES)
            return 0

        lax.fori_loop(0, count, body, 0)

    def quantize(p, l, first, count, q, scale):
        def largest(b, m):
            v = jnp.abs(part[p, l, first + b].reshape(-1, 8, LANES))
            return jnp.maximum(m, jnp.max(v, axis=0))

        m = lax.fori_loop(0, count, largest, jnp.zeros((8, LANES), F32))
        m = jnp.maximum(m, 1e-30)
        scale[0:8] = m * (1.0 / 32767.0)
        inverse = 32767.0 / m

        def body(b, _):
            v = part[p, l, first + b].reshape(-1, 8, LANES) * inverse
            q[b] = jnp.round(v).astype(jnp.int32).astype(jnp.int16).reshape(2 * ROWS, LANES)
            return 0

        lax.fori_loop(0, count, body, 0)

    def z_copies(way, s, l):
        target = up if way == 0 else down
        return (
            remote(zsx.at[way, s, l], zrx.at[way, s, l], z_send.at[way, s, l, 0], z_recv.at[way, s, l, 0], target),
            remote(zs.at[way, s, l], zr.at[way, s, l], z_send.at[way, s, l, 1], z_recv.at[way, s, l, 1], target),
        )

    def x_copies(way, s):
        target = up if way == 0 else down
        if s == 0:
            blocks = pl.ds(0, XA) if way == 0 else pl.ds(XA, NX - XA)
        else:
            blocks = pl.ds(0, NX)
        return (
            remote(xsx.at[way, s], xrx.at[way, s], x_send.at[way, s, 0], x_recv.at[way, s, 0], target),
            remote(xs.at[way, s, blocks], xr.at[way, s, blocks], x_send.at[way, s, 1], x_recv.at[way, s, 1], target),
        )

    def e_copies(p):
        q, r = (fs, fr) if p is LAST else (es.at[p], er.at[p])
        return (
            remote(esx.at[p], erx.at[p], e_send.at[p, 0], e_recv.at[p, 0], pair),
            remote(q, r, e_send.at[p, 1], e_recv.at[p, 1], pair),
        )

    def receive(copies):
        for copy in copies:
            copy.wait_recv()

    def z_receive(p, way, s, l):
        receive(z_copies(way, s, l))
        add(p, l, 0, NZ, zr.at[way, s, l], zrx.at[way, s, l])
        left[p, l] = left[p, l] + zrx[way, s, l, 8:16]

    def x_receive(p, way, s):
        receive(x_copies(way, s))
        first, count = (0, NX) if s > 0 else ((0, XA) if way == 0 else (XA, NX - XA))
        add(p, xl, NZ + first, count, xr.at[way, s, pl.ds(first, count)], xrx.at[way, s])

    def x_emit(p, way, s):
        first, count = (0, NX) if s > 0 else ((0, XA) if way == 0 else (XA, NX - XA))
        quantize(p, xl, NZ + first, count, xs.at[way, s, pl.ds(first, count)], xsx.at[way, s])
        send(x_copies(way, s))

    def e_emit(p):
        quantize(p, 1 - xl, NZ, NX, es.at[p], esx.at[p])
        send(e_copies(p))

    def e_receive(p):
        receive(e_copies(p))
        add(p, xl, NZ, NX, er.at[p], erx.at[p])

    chunks = ((0, 0), (1, 2), (3, 4), (5, 6))


    def z_part(s, way, l):
        p = chunks[s][way]

        if s > 1 or (s == 1 and l == way):
            z_receive(p, way, s - 1, l)
        quantize(p, l, 0, NZ, zs.at[way, s, l], zsx.at[way, s, l])
        zsx[way, s, l, 8:16] = left[p, l]
        for copy in z_copies(way, s, l):
            copy.start()

    def give_all(source, slot, order, target):
        for part_of in order:
            give(source, slot, part_of, target)

    rising, falling = (0, 1, 2), (2, 1, 0)
    for i in range(3):
        give(OWN, Y_M, rising[i], y_up)
        give(OWN, Y_P, falling[i], y_down)
        give(OWN, R_OWN, rising[i], across)
    for part_of in range(3):
        share(OWN, part_of)
    b_copy.wait()
    arrive_sibling(OWN)
    prepare(OWN, places[OWN])
    multiply(OWN, places[OWN])
    e_emit(places[OWN])
    arrive(Y_M, 0)
    give(Y_M, Y_2, 0, y_up)
    for part_of in (2, 1):
        arrive(Y_P, part_of)
        give(Y_P, Y_2, part_of, y_down)
    arrive(R_OWN, 0)
    give(R_OWN, R_M, 0, y_up)
    for part_of in (2, 1):
        arrive(R_OWN, part_of)
        give(R_OWN, R_P, part_of, y_down)
    give_all(R_OWN, R_M, (1, 2), y_up)
    give(R_OWN, R_P, 0, y_down)
    for part_of in (1, 2):
        arrive(Y_M, part_of)
    arrive(Y_P, 0)
    arrive_sibling(Y_M)
    prepare(Y_M, places[Y_M])
    multiply(Y_M, places[Y_M])
    for part_of in range(3):
        arrive(Y_2, part_of)
    e_emit(places[Y_M])
    arrive_sibling(Y_P)
    prepare(Y_P, places[Y_P])
    multiply(Y_P, places[Y_P])
    arrive(R_M, 0)
    give(R_M, R_2, 0, y_up)
    for part_of in (2, 1):
        arrive(R_P, part_of)
        give(R_P, R_2, part_of, y_down)
    e_emit(places[Y_P])
    arrive_sibling(R_OWN)
    prepare(R_OWN, places[R_OWN])
    multiply(R_OWN, places[R_OWN])
    for part_of in (1, 2):
        arrive(R_M, part_of)
    arrive(R_P, 0)
    arrive_sibling(Y_2)
    prepare(Y_2, places[Y_2])
    multiply(Y_2, places[Y_2])
    arrive_sibling(R_M)
    prepare(R_M, places[R_M])
    multiply(R_M, places[R_M], (0, 1))
    for part_of in range(3):
        arrive(R_2, part_of)
    multiply(R_M, places[R_M], (1, 2))
    arrive_sibling(R_P)
    arrive_sibling(R_2)
    keys = [places[n] * 8 + n for n in (R_P, R_2)]
    first, second = jnp.minimum(keys[0], keys[1]), jnp.maximum(keys[0], keys[1])

    def e_late(p):
        early = [places[n] == p for n in EARLY]
        done = functools.reduce(jnp.logical_or, early)

        @pl.when(jnp.logical_not(done))
        def _():
            quantize(p, 1 - xl, NZ, NX, es.at[p], esx.at[p])
            for copy in e_copies(p):
                copy.start()

        late.append((done, p))

    late = []

    def x_step(s):
        if s == 0:
            e_receive(0)
        for way in (0, 1):
            p = chunks[s][way]
            if s > 0:
                e_receive(p)
                x_receive(p, way, s - 1)
            x_emit(p, way, s)

    prepare(first % 8, first // 8)
    multiply(first % 8, first // 8, (0, 1))
    z_part(0, 0, 0)
    z_part(0, 1, 1)
    multiply(first % 8, first // 8, (1, 2))
    e_late(0)
    prepare(second % 8, second // 8)
    multiply(second % 8, second // 8, (0, 1))
    z_part(1, 0, 1)
    z_part(1, 1, 0)
    multiply(second % 8, second // 8, (1, 2))
    for p in range(1, 8):
        e_late(p)
    z_part(1, 0, 0)
    z_part(1, 1, 1)
    x_step(0)
    for l in (0, 1):
        for way in (0, 1):
            z_part(2, way, l)
    x_step(1)
    for way in (0, 1):
        z_part(3, way, 1 - xl)
    x_step(2)
    for way in (0, 1):
        z_part(3, way, xl)
    x_step(3)

    for way in (0, 1):
        z_receive(7, way, 3, 1 - xl)
    quantize(7, 1 - xl, 0, NZ, fs, esx.at[LAST])
    esx[LAST, 8:16] = left[7, 1 - xl]
    send(e_copies(LAST))
    for way in (0, 1):
        z_receive(7, way, 3, xl)
    e_receive(7)
    for way in (0, 1):
        x_receive(7, way, 3)

    def write(b):
        for side in range(2):
            first = (2 * b + side) * LANES
            out_ref[:, first:first + LANES] = part[7, xl, b, side * ROWS:side * ROWS + rows]

    for b in range(NZ, NB):
        write(b)
    receive(e_copies(LAST))
    add(7, xl, 0, NZ, fr, erx.at[LAST])
    for b in range(NZ):
        write(b)
    tmp[0:8] = left[7, xl] + erx[LAST, 8:16]
    out_ref[:, 2 * NB * LANES:] = tmp[...].T[0:rows, 0:tail]

    for done, p in late:
        @pl.when(jnp.logical_not(done))
        def _(p=p):
            for copy in e_copies(p):
                copy.wait_send()
    for s in range(4):
        for way in (0, 1):
            for l in (0, 1) if s > 0 else (way,):
                for copy in z_copies(way, s, l):
                    copy.wait_send()
    for copy in started:
        copy.wait_send()


def on_device(amplitudes, integrals, cd_blocks):
    rows, depth = amplitudes.shape
    width = integrals.shape[1]
    message = (2 * ROWS, LANES)
    dma = pltpu.SemaphoreType.DMA
    return pl.pallas_call(
        kernel,
        out_shape=jax.ShapeDtypeStruct((rows, width), F32),
        in_specs=[
            pl.BlockSpec(memory_space=pltpu.VMEM),
            pl.BlockSpec(memory_space=pltpu.SMEM),
            pl.BlockSpec(memory_space=pl.ANY),
        ],
        out_specs=pl.BlockSpec(memory_space=pltpu.VMEM),
        scratch_shapes=[
            pltpu.VMEM((8, 2, PAD, depth), jnp.bfloat16),
            pltpu.VMEM((8, 2, 16, QUAD), jnp.bfloat16),
            pltpu.VMEM((depth, width), jnp.bfloat16),
            pltpu.VMEM((8, 2, NB) + message, F32),
            pltpu.VMEM((LANES, LANES), F32),
            pltpu.VMEM((8, 2, 8, LANES), F32),
            pltpu.VMEM((2, 4, 2, NZ) + message, jnp.int16),
            pltpu.VMEM((2, 4, 2, NZ) + message, jnp.int16),
            pltpu.VMEM((2, 4, 2, 16, LANES), F32),
            pltpu.VMEM((2, 4, 2, 16, LANES), F32),
            pltpu.VMEM((2, 4, NX) + message, jnp.int16),
            pltpu.VMEM((2, 4, NX) + message, jnp.int16),
            pltpu.VMEM((2, 4, 8, LANES), F32),
            pltpu.VMEM((2, 4, 8, LANES), F32),
            pltpu.VMEM((8, NX) + message, jnp.int16),
            pltpu.VMEM((8, NX) + message, jnp.int16),
            pltpu.VMEM((9, 16, LANES), F32),
            pltpu.VMEM((9, 16, LANES), F32),
            pltpu.VMEM((NZ,) + message, jnp.int16),
            pltpu.VMEM((NZ,) + message, jnp.int16),
            dma(()),
            dma((8, 3, 2)),
            dma((8, 2, 3)),
            dma((2, 4, 2, 2)),
            dma((2, 4, 2, 2)),
            dma((2, 4, 2)),
            dma((2, 4, 2)),
            dma((9, 2)),
            dma((9, 2)),
        ],
        compiler_params=pltpu.CompilerParams(
            collective_id=0, has_side_effects=True, vmem_limit_bytes=56 * 2**20
        ),
    )(amplitudes, cd_blocks, integrals)


def solution(mesh):
    return jax.shard_map(
        on_device,
        mesh=mesh,
        in_specs=(P("blk", "bulk"), P("bulk", "blk"), P("bulk", None)),
        out_specs=P("bulk", "blk"),
        check_vma=False,
    )
```

```python
import functools

import jax
import jax.numpy as jnp
from jax import lax
from jax.experimental import pallas as pl
from jax.experimental.pallas import tpu as pltpu
from jax.sharding import PartitionSpec as P

MESH = pl.DeviceIdType.MESH
F32 = jnp.float32

DELTA = (4, 3, 5, 2, 6, 1, 7, 0)
NZ = 3
NB = 7
NX = NB - NZ
XA = (NX + 1) // 2
LANES = 128
PAD = 112
ROWS = 104
FULL = 96
QUAD = 512
OWN, Y_M, Y_P, Y_2, R_OWN, R_M, R_P, R_2 = range(8)
LAST = 8
EARLY = (OWN, Y_M, Y_P)


def kernel(a_ref, cd_ref, b_hbm, out_ref, abuf, ebuf, b_ref, part, tmp, left, zs, zr, zsx, zrx, xs, xr, xsx, xrx,
           es, er, esx, erx, fs, fr, b_sem, g_send, g_recv, z_send, z_recv, x_send, x_recv, e_send, e_recv):
    rows, depth = a_ref.shape
    tail = b_hbm.shape[1] - 2 * NB * LANES
    blk, bulk = lax.axis_index("blk"), lax.axis_index("bulk")
    y, h, k = blk // 4, (blk // 2) % 2, blk % 2
    z, xl = bulk // 2, bulk % 2

    def at_y(step):
        return (((y + step + 4) % 4) * 4 + h * 2 + k, bulk)

    def at_z(step):
        return (blk, ((z + step + 8) % 8) * 2 + xl)

    up, down = at_z(1), at_z(-1)
    y_up, y_down = at_y(1), at_y(-1)
    across = (y * 4 + (1 - h) * 2 + k, bulk)
    sibling = (y * 4 + h * 2 + (1 - k), bulk)
    pair = (blk, z * 2 + (1 - xl))

    b_copy = pltpu.make_async_copy(b_hbm, b_ref, b_sem)
    b_copy.start()

    barrier = pltpu.get_barrier_semaphore()
    partners = (up, down, y_up, y_down, across, sibling, pair)
    for partner in partners:
        pl.semaphore_signal(barrier, inc=1, device_id=partner, device_id_type=MESH)

    def remote(src, dst, send, recv, target):
        return pltpu.make_async_remote_copy(
            src_ref=src, dst_ref=dst, send_sem=send, recv_sem=recv, device_id=target, device_id_type=MESH
        )

    def place(n):
        source = ((y + (0, -1, 1, 2)[n % 4] + 4) % 4) * 2 + (h if n < 4 else 1 - h)
        d = (source - z + 8) % 8
        return jnp.where(d < 4, 7 - 2 * d, 2 * (d - 4))

    places = [place(n) for n in range(8)]

    per_block = depth // cd_ref.shape[0]
    column = lax.broadcasted_iota(jnp.int32, (1, depth), 1)
    weight = jnp.zeros((1, depth), F32)
    for block in range(cd_ref.shape[0]):
        factor = jnp.where(cd_ref[block, 0] == cd_ref[block, 1], 1.0, 2.0).astype(F32)
        inside = jnp.logical_and(column >= block * per_block, column < (block + 1) * per_block)
        weight = jnp.where(inside, factor, weight)
    tmp[...] = jnp.zeros_like(tmp)
    weighted = a_ref[...].astype(F32) * weight
    main = 2 * NB * LANES
    abuf[OWN, k, 0:FULL, 0:main] = weighted[0:FULL, 0:main].astype(jnp.bfloat16)
    tmp[0:rows, 0:depth - main] = weighted[:, main:]
    ends = tmp[...].T[0:8]
    last = weighted[FULL:rows, 0:main]
    spare = jnp.concatenate([last[:, 3 * QUAD:], ends[0:4], ends[4:8]], axis=1)
    ebuf[OWN, k] = jnp.concatenate(
        [last[:, 0:QUAD], last[:, QUAD:2 * QUAD], last[:, 2 * QUAD:3 * QUAD], spare], axis=0).astype(jnp.bfloat16)
    tmp[...] = jnp.zeros_like(tmp)

    pl.semaphore_wait(barrier, len(partners))

    def half(n, l, part_of):
        if part_of == 2:
            return ebuf.at[n, l]
        return abuf.at[n, l, pl.ds(part_of * (FULL // 2), FULL // 2), pl.ds(0, main)]

    started = []

    def send(copies):
        for copy in copies:
            copy.start()
            started.append(copy)

    def give(source, target_slot, part_of, target):
        send([remote(half(source, k, part_of), half(target_slot, k, part_of), g_send.at[target_slot, part_of, 0],
                     g_recv.at[target_slot, k, part_of], target)])

    def share(n, part_of):
        ref = half(n, k, part_of)
        send([remote(ref, ref, g_send.at[n, part_of, 1], g_recv.at[n, k, part_of], sibling)])

    def arrive(n, part_of):
        ref = half(n, k, part_of)
        remote(ref, ref, g_send.at[n, part_of, 0], g_recv.at[n, k, part_of], sibling).wait_recv()
        share(n, part_of)

    def arrive_sibling(n):
        for part_of in range(3):
            ref = half(n, 1 - k, part_of)
            remote(ref, ref, g_send.at[n, part_of, 1], g_recv.at[n, 1 - k, part_of], sibling).wait_recv()

    def unpack(n):
        for l in range(2):
            e = ebuf[n, l].astype(F32)
            low = jnp.concatenate([e[0:4], e[4:8], e[8:12], e[12:16, 0:main - 3 * QUAD]], axis=1)
            low = jnp.concatenate([low, jnp.zeros((PAD - FULL - 4, main), F32)], axis=0)
            abuf[n, l, FULL:PAD, 0:main] = low.astype(jnp.bfloat16)
            ends = jnp.concatenate([e[12:16, QUAD - 2 * LANES:QUAD - LANES], e[12:16, QUAD - LANES:]], axis=0)
            abuf[n, l, :, main:] = ends.T[0:PAD].astype(jnp.bfloat16)

    def multiply(n, p, sides=(0, 2)):
        lhs = abuf[n].reshape(2 * PAD, depth)
        wide = NB * LANES

        def body(side, _):
            r = jnp.dot(lhs, b_ref[:, pl.ds(pl.multiple_of(side * wide, LANES), wide)], preferred_element_type=F32)
            for l in range(2):
                for j in range(NB):
                    tile = side * NB + j
                    part[p, l, tile // 2, pl.ds(pl.multiple_of(tile % 2 * ROWS, 8), ROWS)] = r[
                        l * PAD:l * PAD + ROWS, j * LANES:(j + 1) * LANES]
            return 0

        lax.fori_loop(sides[0], sides[1], body, 0)

    def prepare(n, p):
        unpack(n)
        r = jnp.dot(abuf[n].reshape(2 * PAD, depth), b_ref[:, main:], preferred_element_type=F32)
        for l in range(2):
            tmp[0:PAD, 0:tail] = r[l * PAD:(l + 1) * PAD]
            left[p, l] = tmp[...].T[0:8]

    def add(p, l, first, count, q, scale):
        factor = scale[0:8]

        def body(b, _):
            more = q[b].astype(F32).reshape(-1, 8, LANES) * factor
            v = part[p, l, first + b].reshape(-1, 8, LANES) + more
            part[p, l, first + b] = v.reshape(2 * ROWS, LANES)
            return 0

        lax.fori_loop(0, count, body, 0)

    def quantize(p, l, first, count, q, scale):
        def largest(b, m):
            v = jnp.abs(part[p, l, first + b].reshape(-1, 8, LANES))
            return jnp.maximum(m, jnp.max(v, axis=0))

        m = lax.fori_loop(0, count, largest, jnp.zeros((8, LANES), F32))
        m = jnp.maximum(m, 1e-30)
        scale[0:8] = m * (1.0 / 32767.0)
        inverse = 32767.0 / m

        def body(b, _):
            v = part[p, l, first + b].reshape(-1, 8, LANES) * inverse
            q[b] = jnp.round(v).astype(jnp.int32).astype(jnp.int16).reshape(2 * ROWS, LANES)
            return 0

        lax.fori_loop(0, count, body, 0)

    def z_copies(way, s, l):
        target = up if way == 0 else down
        return (
            remote(zsx.at[way, s, l], zrx.at[way, s, l], z_send.at[way, s, l, 0], z_recv.at[way, s, l, 0], target),
            remote(zs.at[way, s, l], zr.at[way, s, l], z_send.at[way, s, l, 1], z_recv.at[way, s, l, 1], target),
        )

    def x_copies(way, s):
        target = up if way == 0 else down
        if s == 0:
            blocks = pl.ds(0, XA) if way == 0 else pl.ds(XA, NX - XA)
        else:
            blocks = pl.ds(0, NX)
        return (
            remote(xsx.at[way, s], xrx.at[way, s], x_send.at[way, s, 0], x_recv.at[way, s, 0], target),
            remote(xs.at[way, s, blocks], xr.at[way, s, blocks], x_send.at[way, s, 1], x_recv.at[way, s, 1], target),
        )

    def e_copies(p):
        q, r = (fs, fr) if p is LAST else (es.at[p], er.at[p])
        return (
            remote(esx.at[p], erx.at[p], e_send.at[p, 0], e_recv.at[p, 0], pair),
            remote(q, r, e_send.at[p, 1], e_recv.at[p, 1], pair),
        )

    def receive(copies):
        for copy in copies:
            copy.wait_recv()

    def z_receive(p, way, s, l):
        receive(z_copies(way, s, l))
        add(p, l, 0, NZ, zr.at[way, s, l], zrx.at[way, s, l])
        left[p, l] = left[p, l] + zrx[way, s, l, 8:16]

    def x_receive(p, way, s):
        receive(x_copies(way, s))
        first, count = (0, NX) if s > 0 else ((0, XA) if way == 0 else (XA, NX - XA))
        add(p, xl, NZ + first, count, xr.at[way, s, pl.ds(first, count)], xrx.at[way, s])

    def x_emit(p, way, s):
        first, count = (0, NX) if s > 0 else ((0, XA) if way == 0 else (XA, NX - XA))
        quantize(p, xl, NZ + first, count, xs.at[way, s, pl.ds(first, count)], xsx.at[way, s])
        send(x_copies(way, s))

    def e_emit(p):
        quantize(p, 1 - xl, NZ, NX, es.at[p], esx.at[p])
        send(e_copies(p))

    def e_receive(p):
        receive(e_copies(p))
        add(p, xl, NZ, NX, er.at[p], erx.at[p])

    chunks = ((0, 0), (1, 2), (3, 4), (5, 6))


    def z_part(s, way, l):
        p = chunks[s][way]

        if s > 1 or (s == 1 and l == way):
            z_receive(p, way, s - 1, l)
        quantize(p, l, 0, NZ, zs.at[way, s, l], zsx.at[way, s, l])
        zsx[way, s, l, 8:16] = left[p, l]
        for copy in z_copies(way, s, l):
            copy.start()

    def give_all(source, slot, order, target):
        for part_of in order:
            give(source, slot, part_of, target)

    rising, falling = (0, 1, 2), (2, 1, 0)
    for i in range(3):
        give(OWN, Y_M, rising[i], y_up)
        give(OWN, Y_P, falling[i], y_down)
        give(OWN, R_OWN, rising[i], across)
    for part_of in range(3):
        share(OWN, part_of)
    b_copy.wait()
    arrive_sibling(OWN)
    prepare(OWN, places[OWN])
    multiply(OWN, places[OWN])
    e_emit(places[OWN])
    arrive(Y_M, 0)
    give(Y_M, Y_2, 0, y_up)
    for part_of in (2, 1):
        arrive(Y_P, part_of)
        give(Y_P, Y_2, part_of, y_down)
    arrive(R_OWN, 0)
    give(R_OWN, R_M, 0, y_up)
    for part_of in (2, 1):
        arrive(R_OWN, part_of)
        give(R_OWN, R_P, part_of, y_down)
    give_all(R_OWN, R_M, (1, 2), y_up)
    give(R_OWN, R_P, 0, y_down)
    for part_of in (1, 2):
        arrive(Y_M, part_of)
    arrive(Y_P, 0)
    arrive_sibling(Y_M)
    prepare(Y_M, places[Y_M])
    multiply(Y_M, places[Y_M])
    for part_of in range(3):
        arrive(Y_2, part_of)
    e_emit(places[Y_M])
    arrive_sibling(Y_P)
    prepare(Y_P, places[Y_P])
    multiply(Y_P, places[Y_P])
    arrive(R_M, 0)
    give(R_M, R_2, 0, y_up)
    for part_of in (2, 1):
        arrive(R_P, part_of)
        give(R_P, R_2, part_of, y_down)
    e_emit(places[Y_P])
    arrive_sibling(R_OWN)
    prepare(R_OWN, places[R_OWN])
    multiply(R_OWN, places[R_OWN])
    for part_of in (1, 2):
        arrive(R_M, part_of)
    arrive(R_P, 0)
    arrive_sibling(Y_2)
    prepare(Y_2, places[Y_2])
    multiply(Y_2, places[Y_2])
    arrive_sibling(R_M)
    prepare(R_M, places[R_M])
    multiply(R_M, places[R_M], (0, 1))
    for part_of in range(3):
        arrive(R_2, part_of)
    multiply(R_M, places[R_M], (1, 2))
    arrive_sibling(R_P)
    arrive_sibling(R_2)
    keys = [places[n] * 8 + n for n in (R_P, R_2)]
    first, second = jnp.minimum(keys[0], keys[1]), jnp.maximum(keys[0], keys[1])

    def e_late(p):
        early = [places[n] == p for n in EARLY]
        done = functools.reduce(jnp.logical_or, early)

        @pl.when(jnp.logical_not(done))
        def _():
            quantize(p, 1 - xl, NZ, NX, es.at[p], esx.at[p])
            for copy in e_copies(p):
                copy.start()

        late.append((done, p))

    late = []

    def x_step(s):
        if s == 0:
            e_receive(0)
        for way in (0, 1):
            p = chunks[s][way]
            if s > 0:
                e_receive(p)
                x_receive(p, way, s - 1)
            x_emit(p, way, s)

    prepare(first % 8, first // 8)
    multiply(first % 8, first // 8, (0, 1))
    z_part(0, 0, 0)
    z_part(0, 1, 1)
    multiply(first % 8, first // 8, (1, 2))
    e_late(0)
    prepare(second % 8, second // 8)
    multiply(second % 8, second // 8, (0, 1))
    z_part(1, 0, 1)
    z_part(1, 1, 0)
    multiply(second % 8, second // 8, (1, 2))
    e_late(1)
    e_late(2)
    z_part(1, 0, 0)
    z_part(1, 1, 1)
    for p in range(3, 8):
        e_late(p)
    x_step(0)
    for l in (0, 1):
        for way in (0, 1):
            z_part(2, way, l)
    x_step(1)
    for way in (0, 1):
        z_part(3, way, 1 - xl)
    x_step(2)
    for way in (0, 1):
        z_part(3, way, xl)
    x_step(3)

    for way in (0, 1):
        z_receive(7, way, 3, 1 - xl)
    quantize(7, 1 - xl, 0, NZ, fs, esx.at[LAST])
    esx[LAST, 8:16] = left[7, 1 - xl]
    send(e_copies(LAST))
    for way in (0, 1):
        z_receive(7, way, 3, xl)
    e_receive(7)
    for way in (0, 1):
        x_receive(7, way, 3)

    def write(b):
        for side in range(2):
            first = (2 * b + side) * LANES
            out_ref[:, first:first + LANES] = part[7, xl, b, side * ROWS:side * ROWS + rows]

    for b in range(NZ, NB):
        write(b)
    receive(e_copies(LAST))
    add(7, xl, 0, NZ, fr, erx.at[LAST])
    for b in range(NZ):
        write(b)
    tmp[0:8] = left[7, xl] + erx[LAST, 8:16]
    out_ref[:, 2 * NB * LANES:] = tmp[...].T[0:rows, 0:tail]

    for done, p in late:
        @pl.when(jnp.logical_not(done))
        def _(p=p):
            for copy in e_copies(p):
                copy.wait_send()
    for s in range(4):
        for way in (0, 1):
            for l in (0, 1) if s > 0 else (way,):
                for copy in z_copies(way, s, l):
                    copy.wait_send()
    for copy in started:
        copy.wait_send()


def on_device(amplitudes, integrals, cd_blocks):
    rows, depth = amplitudes.shape
    width = integrals.shape[1]
    message = (2 * ROWS, LANES)
    dma = pltpu.SemaphoreType.DMA
    return pl.pallas_call(
        kernel,
        out_shape=jax.ShapeDtypeStruct((rows, width), F32),
        in_specs=[
            pl.BlockSpec(memory_space=pltpu.VMEM),
            pl.BlockSpec(memory_space=pltpu.SMEM),
            pl.BlockSpec(memory_space=pl.ANY),
        ],
        out_specs=pl.BlockSpec(memory_space=pltpu.VMEM),
        scratch_shapes=[
            pltpu.VMEM((8, 2, PAD, depth), jnp.bfloat16),
            pltpu.VMEM((8, 2, 16, QUAD), jnp.bfloat16),
            pltpu.VMEM((depth, width), jnp.bfloat16),
            pltpu.VMEM((8, 2, NB) + message, F32),
            pltpu.VMEM((LANES, LANES), F32),
            pltpu.VMEM((8, 2, 8, LANES), F32),
            pltpu.VMEM((2, 4, 2, NZ) + message, jnp.int16),
            pltpu.VMEM((2, 4, 2, NZ) + message, jnp.int16),
            pltpu.VMEM((2, 4, 2, 16, LANES), F32),
            pltpu.VMEM((2, 4, 2, 16, LANES), F32),
            pltpu.VMEM((2, 4, NX) + message, jnp.int16),
            pltpu.VMEM((2, 4, NX) + message, jnp.int16),
            pltpu.VMEM((2, 4, 8, LANES), F32),
            pltpu.VMEM((2, 4, 8, LANES), F32),
            pltpu.VMEM((8, NX) + message, jnp.int16),
            pltpu.VMEM((8, NX) + message, jnp.int16),
            pltpu.VMEM((9, 16, LANES), F32),
            pltpu.VMEM((9, 16, LANES), F32),
            pltpu.VMEM((NZ,) + message, jnp.int16),
            pltpu.VMEM((NZ,) + message, jnp.int16),
            dma(()),
            dma((8, 3, 2)),
            dma((8, 2, 3)),
            dma((2, 4, 2, 2)),
            dma((2, 4, 2, 2)),
            dma((2, 4, 2)),
            dma((2, 4, 2)),
            dma((9, 2)),
            dma((9, 2)),
        ],
        compiler_params=pltpu.CompilerParams(
            collective_id=0, has_side_effects=True, vmem_limit_bytes=56 * 2**20
        ),
    )(amplitudes, cd_blocks, integrals)


def solution(mesh):
    return jax.shard_map(
        on_device,
        mesh=mesh,
        in_specs=(P("blk", "bulk"), P("bulk", "blk"), P("bulk", None)),
        out_specs=P("bulk", "blk"),
        check_vma=False,
    )
```
